32 devices in a mesh: row: 4 (over z), col: 8 (over y, x, core).
Axes of the slice: x: 2, y: 2, z: 4, core: 2. Of those that a mesh axis runs over, the one named last changes fastest.
Arguments:
- trailing: bfloat16 [8192, 12288], P('row', 'col'), may hold values from -6 to 6
- low_factor: bfloat16 [2, 8192, 512], P(None, ('row', 'col')), may hold values from -0.1875 to 0.1875
- panel_tops: bfloat16 [2, 512, 12288], P(None, 'row', 'col'), may hold values from -6 to 6
- diag_inverses: bfloat16 [2, 512, 512], replicated, as said below
- link_rows: bfloat16 [512, 512], replicated, may hold values from -0.25 to 0.25
- pivots: int32 [2, 512], replicated, may hold values from 0 to 511, each once within a row
- residual: float32 [1024, 4096], P('row', 'col'), may hold values from -6 to 6
- diagonal: float32 [1024, 4096], P('row', 'col'), may hold values from 0.5 to 2
- coupling: float32 [1024, 4096], P('row', 'col'), may hold values from 0.6 to 1
- basis_cells: int32 [32, 32, 128], P(('row', 'col')), may hold values from 0 to 131071
- basis_weights: float32 [32, 32, 128], P(('row', 'col')), may hold values from 0.1 to 0.4
- coarse_slots: int32 [32, 32, 128], P(('row', 'col')), may hold values from -1 to 383, as said below
Outputs:
- updated: bfloat16 [8192, 12288], P('row', 'col')
- upper_rows: bfloat16 [2, 512, 12288], P(None, None, 'col')
- smoothed: float32 [1024, 4096], P('row', 'col')
- coarse_residual: float32 [12288], P(('row', 'col'))
The draws below stay inside these ranges and needn't reach their ends.
Inputs may be any that keep to these rules, and one draw needn't show every extreme that they name: `coarse_slots`: -1 marks a padded slot. In every block of 128 slots the live slots come first and number at least 32; in every owner's list one source's block is full. Each diag_inverses[p] is unit lower triangular. Each row of pivots is a permutation.
All inputs are finite; a program needn't handle non-finite values.
Results may differ from the reference program's by a relative error of at most 0.0053.
Values may be sent and summed in bfloat16 or wider, within the bound.
A program may use at most 128 MiB of HBM per device.

```python
import math
import jax
import jax.numpy as jnp
from jax import lax

CELLS_X = 256
CELLS_Y = 512
MARGIN = 3
SWEEPS = 3
SLOTS = 128
COARSE_DEV = 384
PANEL = 512
ROWS_DEV = 2048
GRID_X = 1024
GRID_Y = 4096
COARSE = 12288
TRAIL_ROWS = 8192
TRAIL_COLS = 12288
N_ROW = 4
N_COL = 8
DEVICES = 32


def draw_coarse_slots(key, part):
    key = jax.random.fold_in(key, 7)
    device_count = N_ROW * N_COL
    key_live, key_full, key_owner = jax.random.split(key, 3)
    live = jax.random.randint(key_live, (device_count, device_count, 1), SLOTS // 4, SLOTS + 1)
    full_source = jax.random.randint(key_full, (device_count, 1, 1), 0, device_count)
    sources = lax.broadcasted_iota(jnp.int32, (device_count, device_count, 1), 1)
    live = jnp.where(sources == full_source, SLOTS, live)
    positions = lax.broadcasted_iota(jnp.int32, (device_count, device_count, SLOTS), 2)
    owners = jax.random.randint(key_owner, (device_count, device_count, SLOTS), 0, COARSE_DEV)
    return jnp.where(positions < live, owners, -1).astype(jnp.int32)


def draw_diag_inverses(key, part):
    key = jax.random.fold_in(key, 3)
    noise = jnp.clip(jax.random.normal(key, (2, PANEL, PANEL), jnp.float32), -4.0, 4.0)
    below = jnp.tril(jnp.ones((PANEL, PANEL), jnp.float32), -1)
    matrix = jnp.eye(PANEL, dtype=jnp.float32) + below * noise * (0.5 / math.sqrt(PANEL))
    return matrix.astype(jnp.bfloat16)


def plant(array, key, least, largest):
    index_at = [jax.random.randint(jax.random.fold_in(key, axis), (), 0, length) for axis, length in enumerate(array.shape)]
    longest = array.shape.index(max(array.shape))
    neighbour = index_at[:longest] + [(index_at[longest] + 1) % array.shape[longest]] + index_at[longest + 1:]
    return array.at[tuple(index_at)].set(least).at[tuple(neighbour)].set(largest)


def steps_of(rng, extent, shards, least, largest):
    factor_of = 1.0
    for position, blocks in shards:
        steps = jax.random.uniform(jax.random.fold_in(jax.random.fold_in(rng, 6), position), (blocks,), jnp.float32, least / len(shards), largest / len(shards))
        factor_of = factor_of * jnp.repeat(jnp.exp(steps), extent[position] // blocks).reshape((-1,) + (1,) * (len(extent) - 1 - position))
    return factor_of


def normal_values(key, extent, scale, bound, cuts=(), kind=jnp.bfloat16):
    gain = steps_of(key, extent, cuts, -0.22, 0.18) if cuts else 1.0
    entries = jax.random.normal(key, extent, jnp.float32) * scale * gain
    return jnp.minimum(jnp.maximum(entries, -bound), bound).astype(kind)


def setup_inputs(seed: int = 0) -> dict:
    key_list = jax.random.split(jax.random.key(seed), 13)
    trailing = normal_values(key_list[0], (TRAIL_ROWS, TRAIL_COLS), 1.0, 6.0, ((0, 4), (1, 8)))
    low_factor = normal_values(key_list[1], (2, TRAIL_ROWS, PANEL), (2 * PANEL) ** -0.5, 0.1875, ((1, 32),))
    panel_tops = normal_values(key_list[2], (2, PANEL, TRAIL_COLS), 1.0, 6.0, ((1, 4), (2, 8)))
    diag_inverses = draw_diag_inverses(jax.random.fold_in(key_list[12], 71), 0)
    link_rows = normal_values(key_list[4], (PANEL, PANEL), PANEL ** -0.5, 0.25)
    pivots = jax.vmap(lambda own: jax.random.permutation(own, PANEL))(jax.random.split(key_list[5], 2)).reshape((2, PANEL)).astype(jnp.int32)
    residual = normal_values(key_list[6], (GRID_X, GRID_Y), 1.0, 6.0, ((0, 4), (1, 8)), jnp.float32)
    diagonal = jnp.clip(jnp.exp(math.log(2.0) - 1.3862944 * jax.random.uniform(key_list[7], (GRID_X, GRID_Y), jnp.float32) ** steps_of(key_list[7], (GRID_X, GRID_Y), ((0, 4), (1, 8)), -0.2, 0.2)), 0.5, 2.0)
    coupling = jnp.clip(0.6 + 0.39999998 * jax.random.uniform(key_list[8], (GRID_X, GRID_Y), jnp.float32) ** steps_of(key_list[8], (GRID_X, GRID_Y), ((0, 4), (1, 8)), -0.2, 0.2), 0.6, 1.0)
    basis_cells = plant(jax.random.randint(key_list[9], (DEVICES, DEVICES, SLOTS), 0, CELLS_X * CELLS_Y), jax.random.fold_in(key_list[9], 1), 0, (CELLS_X * CELLS_Y) - 1).astype(jnp.int32)
    basis_weights = jnp.clip(0.1 + 0.3 * jax.random.uniform(key_list[10], (DEVICES, DEVICES, SLOTS), jnp.float32) ** steps_of(key_list[10], (DEVICES, DEVICES, SLOTS), ((0, 32),), -0.2, 0.2), 0.1, 0.4)
    coarse_slots = draw_coarse_slots(jax.random.fold_in(key_list[12], 71), 0)
    return {"trailing": trailing, "low_factor": low_factor, "panel_tops": panel_tops, "diag_inverses": diag_inverses, "link_rows": link_rows, "pivots": pivots, "residual": residual, "diagonal": diagonal, "coupling": coupling, "basis_cells": basis_cells, "basis_weights": basis_weights, "coarse_slots": coarse_slots}


def sweeps(residual, inverse, coupling):
    source = residual * inverse
    weight = 0.25 * coupling
    solution = source
    for sweep_number in range(SWEEPS - 1):
        padded = jnp.pad(solution, 1)
        beside = padded[2:, 1:-1] + padded[:-2, 1:-1] + padded[1:-1, 2:] + padded[1:-1, :-2]
        solution = source + weight * beside
    return solution


def smooth(residual, diagonal, coupling):
    padded_res = jnp.pad(residual, MARGIN)
    padded_diag = jnp.pad(diagonal, MARGIN, constant_values=1.0)
    padded_coup = jnp.pad(coupling, MARGIN)
    height = CELLS_X + 2 * MARGIN
    breadth = CELLS_Y + 2 * MARGIN

    def one_block(number):
        row_start = (number // N_COL) * CELLS_X
        col_start = (number % N_COL) * CELLS_Y
        res_block = lax.dynamic_slice(padded_res, (row_start, col_start), (height, breadth))
        diag_block = lax.dynamic_slice(padded_diag, (row_start, col_start), (height, breadth))
        coup_block = lax.dynamic_slice(padded_coup, (row_start, col_start), (height, breadth))
        result = sweeps(res_block, 1.0 / diag_block, coup_block)
        return result[MARGIN:MARGIN + CELLS_X, MARGIN:MARGIN + CELLS_Y]

    blocks = lax.map(one_block, jnp.arange(N_ROW * N_COL, dtype=jnp.int32))
    return blocks.reshape(N_ROW, N_COL, CELLS_X, CELLS_Y).transpose(0, 2, 1, 3).reshape(GRID_X, GRID_Y)


def restrict(residual, basis_cells, basis_weights, coarse_slots):
    device_count = N_ROW * N_COL
    blocks = residual.reshape(N_ROW, CELLS_X, N_COL, CELLS_Y).transpose(0, 2, 1, 3)
    blocks = blocks.reshape(device_count, CELLS_X * CELLS_Y)
    cells = basis_cells.reshape(device_count, device_count * SLOTS)
    values = jnp.take_along_axis(blocks, cells, axis=1) * basis_weights.reshape(device_count, device_count * SLOTS)
    ordered = values.reshape(device_count, device_count, SLOTS).transpose(1, 0, 2)
    owners = jnp.arange(device_count, dtype=jnp.int32).reshape(device_count, 1, 1) * COARSE_DEV
    target = jnp.where(coarse_slots >= 0, owners + coarse_slots, COARSE)
    summed = jax.ops.segment_sum(ordered.reshape(-1), target.reshape(-1), num_segments=COARSE + 1)
    return summed[:COARSE]


def solve_panels(top_rows, diag_inverses, link_rows, pivots):
    upper_one = jnp.dot(diag_inverses[0], jnp.take(top_rows[0], pivots[0], axis=0), preferred_element_type=jnp.float32).astype(jnp.bfloat16)
    panel_two = (top_rows[1].astype(jnp.float32) - jnp.dot(link_rows, upper_one, preferred_element_type=jnp.float32)).astype(jnp.bfloat16)
    upper_two = jnp.dot(diag_inverses[1], jnp.take(panel_two, pivots[1], axis=0), preferred_element_type=jnp.float32).astype(jnp.bfloat16)
    return jnp.stack([upper_one, upper_two])


def reference(trailing, low_factor, panel_tops, diag_inverses, link_rows, pivots, residual, diagonal, coupling, basis_cells, basis_weights, coarse_slots):
    upper_rows = solve_panels(panel_tops, diag_inverses, link_rows, pivots)

    def one_block(number):
        start_row = number * ROWS_DEV
        row_block = lax.dynamic_slice_in_dim(trailing, start_row, ROWS_DEV, 0)
        low_block = lax.dynamic_slice_in_dim(low_factor, start_row, ROWS_DEV, 1)
        total = row_block.astype(jnp.float32) - jnp.dot(low_block[0], upper_rows[0], preferred_element_type=jnp.float32) - jnp.dot(low_block[1], upper_rows[1], preferred_element_type=jnp.float32)
        return total.astype(jnp.bfloat16)

    updated = lax.map(one_block, jnp.arange(N_ROW, dtype=jnp.int32)).reshape(TRAIL_ROWS, TRAIL_COLS)
    smoothed = smooth(residual, diagonal, coupling)
    coarse_residual = restrict(residual, basis_cells, basis_weights, coarse_slots)
    return (updated, upper_rows, smoothed, coarse_residual)
```

```python
import functools

import jax
import jax.numpy as jnp
from jax import lax
from jax.experimental import pallas as pl
from jax.experimental.pallas import tpu as pltpu
from jax.sharding import PartitionSpec as P

MARGIN = 3
COARSE_DEV = 384
CHUNK = 256
ROW_TILE = 512
MESH = pl.DeviceIdType.MESH
F32 = jnp.float32
BF16 = jnp.bfloat16


def flipped(index, mask):
    result, bit = index, 1
    while bit <= mask:
        if mask & bit:
            result = result + bit * (1 - 2 * ((index // bit) % 2))
        bit *= 2
    return result


def masks_of(bits):
    masks = [0]
    for bit in bits:
        masks = masks + [m | bit for m in masks]
    return masks


def low_orders(count):
    bits = [1 << i for i in range(count.bit_length() - 1)]
    far, near = bits[1:], bits[:1]
    return (far + near, far[::-1] + near)


def kernel(
    R,
    C,
    trailing,
    low,
    tops,
    inverses,
    link,
    pivots,
    residual,
    diagonal,
    coupling,
    cells,
    weights,
    slots,
    updated,
    upper,
    smoothed,
    coarse,
    tb,
    lb,
    tr,
    up,
    maps,
    S,
    Wt,
    E1,
    hrow,
    hout,
    hcol,
    parts,
    st1,
    r1,
    r2,
    tops_send,
    tops_recv,
    low_send,
    low_recv,
    hrow_send,
    hrow_recv,
    hcol_send,
    hcol_recv,
    a1_send,
    a1_recv,
    a2_send,
    a2_recv,
    load_sem,
    tops_load,
    upd_sem,
    upp_sem,
):
    me_r, me_c = lax.axis_index("row"), lax.axis_index("col")
    chunks = tb.shape[0]
    kb = tops.shape[1]
    own_x, own_y = residual.shape
    owners = cells.shape[0]

    def remote(src, dst, send, recv, row, col):
        return pltpu.make_async_remote_copy(
            src_ref=src,
            dst_ref=dst,
            send_sem=send,
            recv_sem=recv,
            device_id=(row, col),
            device_id_type=MESH,
        )

    barrier = pltpu.get_barrier_semaphore()
    for i in range(1, R):
        pl.semaphore_signal(
            barrier, inc=1, device_id=(lax.rem(me_r + i, R), me_c), device_id_type=MESH
        )
    for i in range(1, C):
        pl.semaphore_signal(
            barrier, inc=1, device_id=(me_r, lax.rem(me_c + i, C)), device_id_type=MESH
        )

    load_trailing = pltpu.make_async_copy(trailing, tr, load_sem.at[0])
    load_low = [
        pltpu.make_async_copy(low.at[p], lb.at[p, me_c], load_sem.at[1 + p]) for p in range(2)
    ]
    load_tops = [
        pltpu.make_async_copy(
            tops.at[:, :, pl.ds(k * CHUNK, CHUNK)],
            tb.at[k, :, pl.ds(pl.multiple_of(me_r * kb, kb), kb), :],
            tops_load.at[k],
        )
        for k in range(chunks)
    ]

    def tops_copy(way, d, k):
        step = 1 if way == 0 else -1
        block = me_r - step * d
        place = tb.at[k, :, pl.ds(pl.multiple_of(block * kb, kb), kb), :]
        src = tops.at[:, :, pl.ds(k * CHUNK, CHUNK)] if d == 0 else place
        return remote(
            src, place, tops_send.at[way, d, k], tops_recv.at[way, d, k], me_r + step, me_c
        )

    def tops_sends(way, d):
        if way == 0:
            return (me_r - d >= 0) & (me_r + 1 < R)
        return (me_r + d < R) & (me_r - 1 >= 0)

    def tops_start(way, d, k):
        @pl.when(tops_sends(way, d))
        def _():
            tops_copy(way, d, k).start()

    def tops_arrive(way, d, k):
        step = 1 if way == 0 else -1
        block = me_r - step * (d + 1)

        @pl.when((block >= 0) & (block < R))
        def _():
            place = tb.at[k, :, pl.ds(pl.multiple_of(block * kb, kb), kb), :]
            remote(
                place, place, tops_send.at[way, d, k], tops_recv.at[way, d, k], me_r, me_c
            ).wait_recv()

    orders = low_orders(C)

    def low_copy(p, m, bit):
        block = flipped(me_c, m)
        place = lb.at[p, block]
        src = low.at[p] if m == 0 else place
        return remote(
            src, place, low_send.at[p, m | bit], low_recv.at[p, m | bit], me_r, flipped(me_c, bit)
        )

    def low_arrive(p, m):
        place = lb.at[p, flipped(me_c, m)]
        remote(place, place, low_send.at[p, m], low_recv.at[p, m], me_r, me_c).wait_recv()

    def low_forward(p, t):
        order = orders[p]
        for m in masks_of(order[:t]):
            arrived = m | order[t]
            low_arrive(p, arrived)
            for bit in order[t + 1 :]:
                low_copy(p, arrived, bit).start()

    pl.semaphore_wait(barrier, R - 1 + C - 1)
    for k in range(chunks):
        for way in range(2):
            tops_start(way, 0, k)
    for t in range(len(orders[0])):
        for p in range(2):
            low_copy(p, 0, orders[p][t]).start()
    for copy in load_tops + load_low:
        copy.start()
    load_trailing.start()

    mid_y = pl.ds(128, own_y)
    src_own = residual[...] * (1.0 / diagonal[...])
    S[pl.ds(16, own_x), mid_y] = src_own
    Wt[pl.ds(16, own_x), mid_y] = 0.25 * coupling[...]
    arrays = (S, Wt)
    last_x = own_x + 8
    for a in range(2):
        hout[0, a] = arrays[a][pl.ds(16, 8), mid_y]
        hout[1, a] = arrays[a][pl.ds(last_x, 8), mid_y]

    def row_copy(side):
        step = -1 if side == 0 else 1
        return remote(
            hout.at[side], hrow.at[1 - side], hrow_send.at[side], hrow_recv.at[1 - side],
            me_r + step, me_c,
        )

    @pl.when(me_r > 0)
    def _():
        row_copy(0).start()

    @pl.when(me_r < R - 1)
    def _():
        row_copy(1).start()

    whole = residual[...]
    high = whole.astype(BF16)
    rest = whole - high.astype(F32)
    middle = rest.astype(BF16)
    parts[pl.ds(0, own_x), :] = high
    parts[pl.ds(own_x, own_x), :] = middle
    parts[pl.ds(2 * own_x, own_x), :] = (rest - middle.astype(F32)).astype(BF16)
    bits_y = own_y.bit_length() - 1

    def pick(i, carry):
        rows = cells[pl.ds(pl.multiple_of(i * 8, 8), 8), :]
        weight = weights[pl.ds(pl.multiple_of(i * 8, 8), 8), :]
        flat = jnp.concatenate([rows[j : j + 1, :] for j in range(8)], axis=1)
        at_x = lax.shift_right_logical(flat, bits_y)
        at_y = flat & (own_y - 1)
        width = flat.shape[1]
        chosen = (lax.broadcasted_iota(jnp.int32, (own_y, width), 0) == at_y).astype(F32)
        picked = jnp.dot(parts[...], chosen.astype(BF16), preferred_element_type=F32)
        column = (
            picked[:own_x] + picked[own_x : 2 * own_x] + picked[2 * own_x : 3 * own_x]
        )
        here = lax.broadcasted_iota(jnp.int32, (own_x, width), 0) == at_x
        values = jnp.sum(jnp.where(here, column, 0.0), axis=0, keepdims=True)
        for j in range(8):
            index = i * 8 + j
            st1[index % C, index // C] = (
                values[:, j * 128 : (j + 1) * 128] * weight[j : j + 1, :]
            )
        return carry

    lax.fori_loop(0, owners // 8, pick, 0)

    def a1_copy(i):
        return remote(
            st1.at[lax.rem(me_c + i, C)], r1.at[me_c], a1_send.at[i], a1_recv.at[i],
            me_r, lax.rem(me_c + i, C),
        )

    for i in range(1, C):
        a1_copy(i).start()
    r1[me_c] = st1[me_c]

    for p in range(2):
        low_forward(p, 0)

    row_at = lax.broadcasted_iota(jnp.int32, (8, own_y), 0)
    edge_zero = jnp.zeros((8, S.shape[1]), F32)
    for a in range(2):
        arrays[a][pl.ds(0, 8), :] = edge_zero
        arrays[a][pl.ds(own_x + 24, 8), :] = edge_zero
    for side in range(2):
        start = 8 if side == 0 else own_x + 16
        keep = row_at >= 8 - MARGIN if side == 0 else row_at < MARGIN
        present = me_r > 0 if side == 0 else me_r < R - 1

        @pl.when(present)
        def _():
            remote(
                hout.at[side], hrow.at[side], hrow_send.at[side], hrow_recv.at[side], me_r, me_c
            ).wait_recv()
            for a in range(2):
                arrays[a][pl.ds(start, 8), mid_y] = jnp.where(keep, hrow[side, a], 0.0)

        @pl.when(jnp.logical_not(present))
        def _():
            for a in range(2):
                arrays[a][pl.ds(start, 8), mid_y] = jnp.zeros((8, own_y), F32)

    tall = own_x + 16
    lane = lax.broadcasted_iota(jnp.int32, (tall, 128), 1)
    left_tile, right_tile = pl.ds(0, 128), pl.ds(128 + own_y, 128)
    first_tile, last_tile = pl.ds(128, 128), pl.ds(own_y, 128)
    span = pl.ds(8, tall)
    hcol[0] = jnp.where(
        lane < MARGIN, S[span, first_tile], pltpu.roll(Wt[span, first_tile], 8, 1)
    )
    hcol[1] = jnp.where(
        lane >= 128 - MARGIN, S[span, last_tile], pltpu.roll(Wt[span, last_tile], 120, 1)
    )

    def col_copy(side):
        step = -1 if side == 0 else 1
        return remote(
            hcol.at[side], hcol.at[3 - side], hcol_send.at[side], hcol_recv.at[1 - side],
            me_r, me_c + step,
        )

    @pl.when(me_c > 0)
    def _():
        col_copy(0).start()

    @pl.when(me_c < C - 1)
    def _():
        col_copy(1).start()

    count = inverses.shape[1]
    for p in range(2):
        permuter = (
            lax.broadcasted_iota(jnp.int32, (count, count), 0) == pivots[p : p + 1, :]
        ).astype(F32).astype(BF16)
        maps[p] = lax.dot_general(
            inverses[p], permuter, (((1,), (1,)), ((), ())), preferred_element_type=F32
        ).astype(BF16)

    for side in range(2):
        present = me_c > 0 if side == 0 else me_c < C - 1
        tile = left_tile if side == 0 else right_tile
        keep = lane >= 128 - MARGIN if side == 0 else lane < MARGIN

        @pl.when(present)
        def _():
            remote(
                hcol.at[side], hcol.at[2 + side], hcol_send.at[side], hcol_recv.at[side],
                me_r, me_c,
            ).wait_recv()
            got = hcol[2 + side]
            S[span, tile] = jnp.where(keep, got, 0.0)
            Wt[span, tile] = jnp.where(keep, pltpu.roll(got, 8 if side == 0 else 120, 1), 0.0)

        @pl.when(jnp.logical_not(present))
        def _():
            S[span, tile] = jnp.zeros((tall, 128), F32)
            Wt[span, tile] = jnp.zeros((tall, 128), F32)

    breadth = S.shape[1]

    def beside(ref, base):
        block = ref[pl.ds(pl.multiple_of(base - 8, 8), 32), :]
        above = pltpu.roll(block, 1, 0)[8:24]
        below = pltpu.roll(block, 31, 0)[8:24]
        middle_rows = block[8:24]
        return (
            above
            + below
            + pltpu.roll(middle_rows, breadth - 1, 1)
            + pltpu.roll(middle_rows, 1, 1)
        )

    E1[pl.ds(0, 8), :] = edge_zero
    E1[pl.ds(own_x + 24, 8), :] = edge_zero

    def first_sweep(i, carry):
        base = pl.multiple_of(8 + i * 16, 8)
        here = pl.ds(base, 16)
        E1[here, :] = S[here, :] + Wt[here, :] * beside(S, base)
        return carry

    lax.fori_loop(0, tall // 16, first_sweep, 0)

    def second_sweep(i, carry):
        base = pl.multiple_of(16 + i * 16, 16)
        here = pl.ds(base, 16)
        final = S[here, :] + Wt[here, :] * beside(E1, base)
        smoothed[pl.ds(pl.multiple_of(i * 16, 16), 16), :] = final[:, 128 : 128 + own_y]
        return carry

    lax.fori_loop(0, own_x // 16, second_sweep, 0)

    for i in range(1, C):
        remote(
            st1.at[0], r1.at[lax.rem(me_c + C - i, C)], a1_send.at[i], a1_recv.at[i], me_r, me_c
        ).wait_recv()

    def a2_copy(i):
        row = lax.rem(me_r + i, R)
        return remote(
            r1.at[:, row], r2.at[pl.ds(me_r * C, C)], a2_send.at[i], a2_recv.at[i], row, me_c
        )

    for i in range(1, R):
        a2_copy(i).start()
    for c in range(C):
        r2[me_r * C + c] = r1[c, me_r]

    for k in range(chunks):
        for way in range(2):
            tops_arrive(way, 0, k)
            if R > 2:
                tops_start(way, 1, k)

    for i in range(1, R):
        remote(
            r1.at[:, 0], r2.at[pl.ds(lax.rem(me_r + R - i, R) * C, C)], a2_send.at[i],
            a2_recv.at[i], me_r, me_c,
        ).wait_recv()

    unknown = lax.broadcasted_iota(jnp.int32, (COARSE_DEV, 128), 0)

    def add_rows(i, total):
        rows = slots[pl.ds(pl.multiple_of(i * 8, 8), 8), :]
        for j in range(8):
            total = total + jnp.where(unknown == rows[j : j + 1, :], r2[i * 8 + j], 0.0)
        return total

    total = lax.fori_loop(0, owners // 8, add_rows, jnp.zeros((COARSE_DEV, 128), F32))
    coarse[...] = jnp.sum(jnp.transpose(total), axis=0, keepdims=True)

    for t in range(1, len(orders[0])):
        for p in range(2):
            low_forward(p, t)
    for copy in load_low + load_tops:
        copy.wait()
    load_trailing.wait()
    for d in range(1, R - 2):
        for k in range(chunks):
            for way in range(2):
                tops_arrive(way, d, k)
                tops_start(way, d + 1, k)

    tile_rows = lb.shape[2]
    upd_copies, upp_copies = [], []
    for k in range(chunks):
        if R > 2:
            for way in range(2):
                tops_arrive(way, R - 2, k)
        columns = pl.ds(k * CHUNK, CHUNK)
        one = jnp.dot(maps[0], tb[k, 0], preferred_element_type=F32).astype(BF16)
        up[0, :, columns] = one
        two = (
            tb[k, 1].astype(F32) - jnp.dot(link[...], one, preferred_element_type=F32)
        ).astype(BF16)
        up[1, :, columns] = jnp.dot(maps[1], two, preferred_element_type=F32).astype(BF16)
        copy = pltpu.make_async_copy(
            up.at[:, :, columns], upper.at[:, :, columns], upp_sem.at[k]
        )
        copy.start()
        upp_copies.append(copy)

        def apply(i, carry):
            rows = pl.ds(pl.multiple_of(i * tile_rows, tile_rows), tile_rows)
            tr[rows, columns] = (
                tr[rows, columns].astype(F32)
                - jnp.dot(lb[0, i], up[0, :, columns], preferred_element_type=F32)
                - jnp.dot(lb[1, i], up[1, :, columns], preferred_element_type=F32)
            ).astype(BF16)
            return carry

        lax.fori_loop(0, C, apply, 0)
        copy = pltpu.make_async_copy(tr.at[:, columns], updated.at[:, columns], upd_sem.at[k])
        copy.start()
        upd_copies.append(copy)

    for d in range(R - 1):
        for k in range(chunks):
            for way in range(2):

                @pl.when(tops_sends(way, d))
                def _():
                    tops_copy(way, d, k).wait_send()

    for p in range(2):
        for t, bit in enumerate(orders[p]):
            for m in masks_of(orders[p][:t]):
                low_copy(p, m, bit).wait_send()
    for side, present in enumerate((me_r > 0, me_r < R - 1)):

        @pl.when(present)
        def _():
            row_copy(side).wait_send()

    for side, present in enumerate((me_c > 0, me_c < C - 1)):

        @pl.when(present)
        def _():
            col_copy(side).wait_send()

    for i in range(1, C):
        a1_copy(i).wait_send()
    for i in range(1, R):
        a2_copy(i).wait_send()
    for copy in upp_copies + upd_copies:
        copy.wait()


def shards(R, C, trailing, low_factor, panel_tops, diag_inverses, link_rows, pivots, residual,
           diagonal, coupling, basis_cells, basis_weights, coarse_slots):
    rows, columns = trailing.shape
    panel = diag_inverses.shape[1]
    own_x, own_y = residual.shape
    chunks = columns // CHUNK
    devices = R * C
    any_spec = pl.BlockSpec(memory_space=pl.ANY)
    vmem = pl.BlockSpec(memory_space=pltpu.VMEM)
    dma = pltpu.SemaphoreType.DMA
    updated, upper_rows, smoothed, coarse = pl.pallas_call(
        functools.partial(kernel, R, C),
        out_shape=(
            jax.ShapeDtypeStruct((rows, columns), BF16),
            jax.ShapeDtypeStruct((2, panel, columns), BF16),
            jax.ShapeDtypeStruct((own_x, own_y), F32),
            jax.ShapeDtypeStruct((1, COARSE_DEV), F32),
        ),
        in_specs=[any_spec] * 3 + [vmem] * 9,
        out_specs=(any_spec, any_spec, vmem, vmem),
        scratch_shapes=[
            pltpu.VMEM((chunks, 2, panel, CHUNK), BF16),
            pltpu.VMEM((2, C, low_factor.shape[1], panel), BF16),
            pltpu.VMEM((rows, columns), BF16),
            pltpu.VMEM((2, panel, columns), BF16),
            pltpu.VMEM((2, panel, panel), BF16),
            pltpu.VMEM((own_x + 32, own_y + 256), F32),
            pltpu.VMEM((own_x + 32, own_y + 256), F32),
            pltpu.VMEM((own_x + 32, own_y + 256), F32),
            pltpu.VMEM((2, 2, 8, own_y), F32),
            pltpu.VMEM((2, 2, 8, own_y), F32),
            pltpu.VMEM((4, own_x + 16, 128), F32),
            pltpu.VMEM((3 * own_x, own_y), BF16),
            pltpu.VMEM((C, R, 1, 128), F32),
            pltpu.VMEM((C, R, 1, 128), F32),
            pltpu.VMEM((devices, 1, 128), F32),
            dma((2, R - 1, chunks)),
            dma((2, R - 1, chunks)),
            dma((2, C)),
            dma((2, C)),
            dma((2,)),
            dma((2,)),
            dma((2,)),
            dma((2,)),
            dma((C,)),
            dma((C,)),
            dma((R,)),
            dma((R,)),
            dma((3,)),
            dma((chunks,)),
            dma((chunks,)),
            dma((chunks,)),
        ],
        compiler_params=pltpu.CompilerParams(
            collective_id=0, has_side_effects=True, vmem_limit_bytes=56 * 1024 * 1024
        ),
        cost_estimate=pl.CostEstimate(
            flops=2 * rows * columns * 2 * panel, bytes_accessed=4 * rows * columns,
            transcendentals=0,
        ),
    )(
        trailing, low_factor, panel_tops, diag_inverses, link_rows, pivots, residual, diagonal,
        coupling, basis_cells[0], basis_weights[0], coarse_slots[0],
    )
    return updated, upper_rows, smoothed, coarse.reshape(-1)


def solution(mesh):
    return jax.shard_map(
        functools.partial(shards, mesh.shape["row"], mesh.shape["col"]),
        mesh=mesh,
        in_specs=(
            P("row", "col"),
            P(None, ("row", "col"), None),
            P(None, "row", "col"),
            P(),
            P(),
            P(),
            P("row", "col"),
            P("row", "col"),
            P("row", "col"),
            P(("row", "col"), None, None),
            P(("row", "col"), None, None),
            P(("row", "col"), None, None),
        ),
        out_specs=(P("row", "col"), P(None, None, "col"), P("row", "col"), P(("row", "col"))),
        check_vma=False,
    )
```

```python
import functools

import jax
import jax.numpy as jnp
from jax import lax
from jax.experimental import pallas as pl
from jax.experimental.pallas import tpu as pltpu
from jax.sharding import PartitionSpec as P

MARGIN = 3
COARSE_DEV = 384
CHUNK = 256
PARTS = 8
ROW_TILE = 1024
MESH = pl.DeviceIdType.MESH
F32 = jnp.float32
BF16 = jnp.bfloat16


def flipped(index, mask):
    result, bit = index, 1
    while bit <= mask:
        if mask & bit:
            result = result + bit * (1 - 2 * ((index // bit) % 2))
        bit *= 2
    return result


def masks_of(bits):
    masks = [0]
    for bit in bits:
        masks = masks + [m | bit for m in masks]
    return masks


def low_orders(count):
    bits = [1 << i for i in range(count.bit_length() - 1)]
    far, near = bits[1:], bits[:1]
    return (far + near, far[::-1] + near)


def kernel(
    R,
    C,
    trailing,
    low,
    tops,
    inverses_in,
    link_in,
    pivots_in,
    residual_in,
    diagonal_in,
    coupling_in,
    cells_in,
    weights_in,
    slots_in,
    updated,
    upper,
    smoothed_out,
    coarse_out,
    inverses,
    link,
    pivots,
    residual,
    diagonal,
    coupling,
    cells,
    weights,
    slots,
    smoothed,
    coarse,
    tb,
    lb,
    tr,
    up,
    maps,
    S,
    Wt,
    E1,
    hrow,
    hout,
    hcol,
    parts,
    st1,
    r1,
    r2,
    tops_send,
    tops_recv,
    low_send,
    low_recv,
    hrow_send,
    hrow_recv,
    hcol_send,
    hcol_recv,
    a1_send,
    a1_recv,
    a2_send,
    a2_recv,
    load_sem,
    tops_load,
    upd_sem,
    upp_sem,
    small_sem,
    out_sem,
):
    me_r, me_c = lax.axis_index("row"), lax.axis_index("col")
    chunks = tb.shape[0]
    kb = tops.shape[1]
    own_x, own_y = residual.shape
    owners = cells.shape[0]

    def remote(src, dst, send, recv, row, col):
        return pltpu.make_async_remote_copy(
            src_ref=src,
            dst_ref=dst,
            send_sem=send,
            recv_sem=recv,
            device_id=(row, col),
            device_id_type=MESH,
        )

    barrier = pltpu.get_barrier_semaphore()
    for i in range(1, R):
        pl.semaphore_signal(
            barrier, inc=1, device_id=(lax.rem(me_r + i, R), me_c), device_id_type=MESH
        )
    for i in range(1, C):
        pl.semaphore_signal(
            barrier, inc=1, device_id=(me_r, lax.rem(me_c + i, C)), device_id_type=MESH
        )

    ready = updated.shape[1]
    load_trailing = pltpu.make_async_copy(trailing.at[:, pl.ds(0, ready)], tr, load_sem.at[0])
    small = [
        pltpu.make_async_copy(source, target, small_sem.at[i])
        for i, (source, target) in enumerate(
            (
                (residual_in, residual),
                (diagonal_in, diagonal),
                (coupling_in, coupling),
                (cells_in, cells),
                (weights_in, weights),
                (inverses_in, inverses),
                (pivots_in, pivots),
                (slots_in, slots),
                (link_in, link),
            )
        )
    ]
    load_low = [
        pltpu.make_async_copy(low.at[p], lb.at[p, me_c], load_sem.at[1 + p]) for p in range(2)
    ]
    load_tops = [
        pltpu.make_async_copy(
            tops.at[:, :, pl.ds(k * CHUNK, CHUNK)],
            tb.at[k, :, pl.ds(pl.multiple_of(me_r * kb, kb), kb), :],
            tops_load.at[k],
        )
        for k in range(chunks)
    ]

    def tops_copy(way, d, k):
        step = 1 if way == 0 else -1
        block = me_r - step * d
        place = tb.at[k, :, pl.ds(pl.multiple_of(block * kb, kb), kb), :]
        src = tops.at[:, :, pl.ds(k * CHUNK, CHUNK)] if d == 0 else place
        return remote(
            src, place, tops_send.at[way, d, k], tops_recv.at[way, d, k], me_r + step, me_c
        )

    def tops_sends(way, d):
        if way == 0:
            return (me_r - d >= 0) & (me_r + 1 < R)
        return (me_r + d < R) & (me_r - 1 >= 0)

    def tops_start(way, d, k):
        @pl.when(tops_sends(way, d))
        def _():
            tops_copy(way, d, k).start()

    def tops_arrive(way, d, k):
        step = 1 if way == 0 else -1
        block = me_r - step * (d + 1)

        @pl.when((block >= 0) & (block < R))
        def _():
            place = tb.at[k, :, pl.ds(pl.multiple_of(block * kb, kb), kb), :]
            remote(
                place, place, tops_send.at[way, d, k], tops_recv.at[way, d, k], me_r, me_c
            ).wait_recv()

    orders = low_orders(C)

    def low_copy(p, m, bit):
        block = flipped(me_c, m)
        place = lb.at[p, block]
        src = low.at[p] if m == 0 else place
        return remote(
            src, place, low_send.at[p, m | bit], low_recv.at[p, m | bit], me_r, flipped(me_c, bit)
        )

    def low_arrive(p, m):
        place = lb.at[p, flipped(me_c, m)]
        remote(place, place, low_send.at[p, m], low_recv.at[p, m], me_r, me_c).wait_recv()

    def low_forward(p, t):
        order = orders[p]
        for m in masks_of(order[:t]):
            arrived = m | order[t]
            low_arrive(p, arrived)
            for bit in order[t + 1 :]:
                low_copy(p, arrived, bit).start()

    for copy in small[:5]:
        copy.start()
    pl.semaphore_wait(barrier, R - 1 + C - 1)
    for k in range(chunks):
        for way in range(2):
            tops_start(way, 0, k)
    for t in range(len(orders[0])):
        for p in range(2):
            low_copy(p, 0, orders[p][t]).start()
    for copy in small[5:] + load_tops + load_low:
        copy.start()
    load_trailing.start()

    for copy in small[:3]:
        copy.wait()
    mid_y = pl.ds(128, own_y)
    src_own = residual[...] * (1.0 / diagonal[...])
    S[pl.ds(16, own_x), mid_y] = src_own
    Wt[pl.ds(16, own_x), mid_y] = 0.25 * coupling[...]
    arrays = (S, Wt)
    last_x = own_x + 8
    for a in range(2):
        hout[0, a] = arrays[a][pl.ds(16, 8), mid_y]
        hout[1, a] = arrays[a][pl.ds(last_x, 8), mid_y]

    def row_copy(side):
        step = -1 if side == 0 else 1
        return remote(
            hout.at[side], hrow.at[1 - side], hrow_send.at[side], hrow_recv.at[1 - side],
            me_r + step, me_c,
        )

    @pl.when(me_r > 0)
    def _():
        row_copy(0).start()

    @pl.when(me_r < R - 1)
    def _():
        row_copy(1).start()

    whole = residual[...]
    high = whole.astype(BF16)
    rest = whole - high.astype(F32)
    middle = rest.astype(BF16)
    parts[pl.ds(0, own_x), :] = high
    parts[pl.ds(own_x, own_x), :] = middle
    parts[pl.ds(2 * own_x, own_x), :] = (rest - middle.astype(F32)).astype(BF16)
    bits_y = own_y.bit_length() - 1

    def pick(i, carry):
        rows = cells[pl.ds(pl.multiple_of(i * 8, 8), 8), :]
        weight = weights[pl.ds(pl.multiple_of(i * 8, 8), 8), :]
        flat = jnp.concatenate([rows[j : j + 1, :] for j in range(8)], axis=1)
        at_x = lax.shift_right_logical(flat, bits_y)
        at_y = flat & (own_y - 1)
        width = flat.shape[1]
        chosen = (lax.broadcasted_iota(jnp.int32, (own_y, width), 0) == at_y).astype(F32)
        picked = jnp.dot(parts[...], chosen.astype(BF16), preferred_element_type=F32)
        column = (
            picked[:own_x] + picked[own_x : 2 * own_x] + picked[2 * own_x : 3 * own_x]
        )
        here = lax.broadcasted_iota(jnp.int32, (own_x, width), 0) == at_x
        values = jnp.sum(jnp.where(here, column, 0.0), axis=0, keepdims=True)
        for j in range(8):
            index = i * 8 + j
            st1[index % C, index // C] = (
                values[:, j * 128 : (j + 1) * 128] * weight[j : j + 1, :]
            )
        return carry

    for copy in small[3:5]:
        copy.wait()
    lax.fori_loop(0, owners // 8, pick, 0)

    def a1_copy(i):
        return remote(
            st1.at[lax.rem(me_c + i, C)], r1.at[me_c], a1_send.at[i], a1_recv.at[i],
            me_r, lax.rem(me_c + i, C),
        )

    for i in range(1, C):
        a1_copy(i).start()
    r1[me_c] = st1[me_c]

    for p in range(2):
        low_forward(p, 0)

    passed = [0]

    def tops_pass(number):
        for k in range(passed[0], min(passed[0] + number, chunks)):
            for way in range(2):
                tops_arrive(way, 0, k)
                if R > 2:
                    tops_start(way, 1, k)
        passed[0] = min(passed[0] + number, chunks)

    tops_pass(1)

    row_at = lax.broadcasted_iota(jnp.int32, (8, own_y), 0)
    edge_zero = jnp.zeros((8, S.shape[1]), F32)
    for a in range(2):
        arrays[a][pl.ds(0, 8), :] = edge_zero
        arrays[a][pl.ds(own_x + 24, 8), :] = edge_zero
    for side in range(2):
        start = 8 if side == 0 else own_x + 16
        keep = row_at >= 8 - MARGIN if side == 0 else row_at < MARGIN
        present = me_r > 0 if side == 0 else me_r < R - 1

        @pl.when(present)
        def _():
            remote(
                hout.at[side], hrow.at[side], hrow_send.at[side], hrow_recv.at[side], me_r, me_c
            ).wait_recv()
            for a in range(2):
                arrays[a][pl.ds(start, 8), mid_y] = jnp.where(keep, hrow[side, a], 0.0)

        @pl.when(jnp.logical_not(present))
        def _():
            for a in range(2):
                arrays[a][pl.ds(start, 8), mid_y] = jnp.zeros((8, own_y), F32)

    tall = own_x + 16
    lane = lax.broadcasted_iota(jnp.int32, (tall, 128), 1)
    left_tile, right_tile = pl.ds(0, 128), pl.ds(128 + own_y, 128)
    first_tile, last_tile = pl.ds(128, 128), pl.ds(own_y, 128)
    span = pl.ds(8, tall)
    hcol[0] = jnp.where(
        lane < MARGIN, S[span, first_tile], pltpu.roll(Wt[span, first_tile], 8, 1)
    )
    hcol[1] = jnp.where(
        lane >= 128 - MARGIN, S[span, last_tile], pltpu.roll(Wt[span, last_tile], 120, 1)
    )

    def col_copy(side):
        step = -1 if side == 0 else 1
        return remote(
            hcol.at[side], hcol.at[3 - side], hcol_send.at[side], hcol_recv.at[1 - side],
            me_r, me_c + step,
        )

    @pl.when(me_c > 0)
    def _():
        col_copy(0).start()

    @pl.when(me_c < C - 1)
    def _():
        col_copy(1).start()

    tops_pass(2)

    for copy in small[5:7]:
        copy.wait()
    count = inverses.shape[1]
    for p in range(2):
        permuter = (
            lax.broadcasted_iota(jnp.int32, (count, count), 0) == pivots[p : p + 1, :]
        ).astype(F32).astype(BF16)
        maps[p] = lax.dot_general(
            inverses[p], permuter, (((1,), (1,)), ((), ())), preferred_element_type=F32
        ).astype(BF16)

    for side in range(2):
        present = me_c > 0 if side == 0 else me_c < C - 1
        tile = left_tile if side == 0 else right_tile
        keep = lane >= 128 - MARGIN if side == 0 else lane < MARGIN

        @pl.when(present)
        def _():
            remote(
                hcol.at[side], hcol.at[2 + side], hcol_send.at[side], hcol_recv.at[side],
                me_r, me_c,
            ).wait_recv()
            got = hcol[2 + side]
            S[span, tile] = jnp.where(keep, got, 0.0)
            Wt[span, tile] = jnp.where(keep, pltpu.roll(got, 8 if side == 0 else 120, 1), 0.0)

        @pl.when(jnp.logical_not(present))
        def _():
            S[span, tile] = jnp.zeros((tall, 128), F32)
            Wt[span, tile] = jnp.zeros((tall, 128), F32)

    breadth = S.shape[1]

    def beside(ref, base):
        block = ref[pl.ds(pl.multiple_of(base - 8, 8), 32), :]
        above = pltpu.roll(block, 1, 0)[8:24]
        below = pltpu.roll(block, 31, 0)[8:24]
        middle_rows = block[8:24]
        return (
            above
            + below
            + pltpu.roll(middle_rows, breadth - 1, 1)
            + pltpu.roll(middle_rows, 1, 1)
        )

    E1[pl.ds(0, 8), :] = edge_zero
    E1[pl.ds(own_x + 24, 8), :] = edge_zero

    def first_sweep(i, carry):
        base = pl.multiple_of(8 + i * 16, 8)
        here = pl.ds(base, 16)
        E1[here, :] = S[here, :] + Wt[here, :] * beside(S, base)
        return carry

    lax.fori_loop(0, tall // 16, first_sweep, 0)

    def second_sweep(i, carry):
        base = pl.multiple_of(16 + i * 16, 16)
        here = pl.ds(base, 16)
        final = S[here, :] + Wt[here, :] * beside(E1, base)
        smoothed[pl.ds(pl.multiple_of(i * 16, 16), 16), :] = final[:, 128 : 128 + own_y]
        return carry

    lax.fori_loop(0, own_x // 16, second_sweep, 0)
    outs = [pltpu.make_async_copy(smoothed, smoothed_out, out_sem.at[0])]
    outs[0].start()

    for i in range(1, C):
        remote(
            st1.at[0], r1.at[lax.rem(me_c + C - i, C)], a1_send.at[i], a1_recv.at[i], me_r, me_c
        ).wait_recv()

    def a2_copy(i):
        row = lax.rem(me_r + i, R)
        return remote(
            r1.at[:, row], r2.at[pl.ds(me_r * C, C)], a2_send.at[i], a2_recv.at[i], row, me_c
        )

    for i in range(1, R):
        a2_copy(i).start()
    for c in range(C):
        r2[me_r * C + c] = r1[c, me_r]

    tops_pass(chunks)

    for i in range(1, R):
        remote(
            r1.at[:, 0], r2.at[pl.ds(lax.rem(me_r + R - i, R) * C, C)], a2_send.at[i],
            a2_recv.at[i], me_r, me_c,
        ).wait_recv()

    small[7].wait()
    unknown = lax.broadcasted_iota(jnp.int32, (COARSE_DEV, 128), 0)

    def add_rows(i, total):
        rows = slots[pl.ds(pl.multiple_of(i * 8, 8), 8), :]
        for j in range(8):
            total = total + jnp.where(unknown == rows[j : j + 1, :], r2[i * 8 + j], 0.0)
        return total

    total = lax.fori_loop(0, owners // 8, add_rows, jnp.zeros((COARSE_DEV, 128), F32))
    coarse[...] = jnp.sum(jnp.transpose(total), axis=0, keepdims=True)
    outs.append(pltpu.make_async_copy(coarse, coarse_out, out_sem.at[1]))
    outs[1].start()

    for t in range(1, len(orders[0])):
        for p in range(2):
            low_forward(p, t)
    for copy in load_low + load_tops:
        copy.wait()
    load_trailing.wait()
    small[8].wait()
    for d in range(1, R - 2):
        for k in range(chunks):
            for way in range(2):
                tops_arrive(way, d, k)
                tops_start(way, d + 1, k)

    held = lb.shape[2]
    tile_rows = min(ROW_TILE, tr.shape[0])
    group = tile_rows // held
    depth = lb.shape[3]
    upd_copies, upp_copies = [], []
    for k in range(chunks):
        if R > 2:
            for way in range(2):
                tops_arrive(way, R - 2, k)
        columns = pl.ds(k * CHUNK, CHUNK)
        one = jnp.dot(maps[0], tb[k, 0], preferred_element_type=F32).astype(BF16)
        up[0, :, columns] = one
        two = (
            tb[k, 1].astype(F32) - jnp.dot(link[...], one, preferred_element_type=F32)
        ).astype(BF16)
        up[1, :, columns] = jnp.dot(maps[1], two, preferred_element_type=F32).astype(BF16)
        copy = pltpu.make_async_copy(
            up.at[:, :, columns], upper.at[:, :, columns], upp_sem.at[k]
        )
        copy.start()
        upp_copies.append(copy)


        def apply(i, carry):
            rows = pl.ds(pl.multiple_of(i * tile_rows, tile_rows), tile_rows)
            blocks = pl.ds(i * group, group)
            tr[rows, columns] = (
                tr[rows, columns].astype(F32)
                - jnp.dot(
                    lb[0, blocks].reshape(tile_rows, depth),
                    up[0, :, columns],
                    preferred_element_type=F32,
                )
                - jnp.dot(
                    lb[1, blocks].reshape(tile_rows, depth),
                    up[1, :, columns],
                    preferred_element_type=F32,
                )
            ).astype(BF16)
            return carry

        lax.fori_loop(0, tr.shape[0] // tile_rows, apply, 0)
        copy = pltpu.make_async_copy(tr.at[:, columns], updated.at[:, columns], upd_sem.at[k])
        copy.start()
        upd_copies.append(copy)

    for d in range(R - 1):
        for k in range(chunks):
            for way in range(2):

                @pl.when(tops_sends(way, d))
                def _():
                    tops_copy(way, d, k).wait_send()

    for p in range(2):
        for t, bit in enumerate(orders[p]):
            for m in masks_of(orders[p][:t]):
                low_copy(p, m, bit).wait_send()
    for side, present in enumerate((me_r > 0, me_r < R - 1)):

        @pl.when(present)
        def _():
            row_copy(side).wait_send()

    for side, present in enumerate((me_c > 0, me_c < C - 1)):

        @pl.when(present)
        def _():
            col_copy(side).wait_send()

    for i in range(1, C):
        a1_copy(i).wait_send()
    for i in range(1, R):
        a2_copy(i).wait_send()
    for copy in upp_copies + upd_copies + outs:
        copy.wait()


def finish(
    partial, upper_in, smoothed_in, coarse_in,
    updated, upper, smoothed, coarse,
    pv, uv, sv, load_sem, copy_sem,
):
    part = partial.shape[0] // PARTS
    pieces = [
        (partial.at[here], pv.at[here], updated.at[here])
        for here in (pl.ds(i * part, part) for i in range(PARTS))
    ]
    pieces += [(upper_in.at[p], uv.at[p], upper.at[p]) for p in range(2)]
    pieces.append((smoothed_in, sv, smoothed))
    moves = [
        (
            pltpu.make_async_copy(source, through, load_sem.at[i]),
            pltpu.make_async_copy(through, target, copy_sem.at[i]),
        )
        for i, (source, through, target) in enumerate(pieces)
    ]
    for load, _ in moves:
        load.start()
    coarse[...] = coarse_in[0, :]
    for load, store in moves:
        load.wait()
        store.start()
    for _, store in moves:
        store.wait()


def shards(R, C, trailing, low_factor, panel_tops, diag_inverses, link_rows, pivots, residual,
           diagonal, coupling, basis_cells, basis_weights, coarse_slots):
    rows, columns = trailing.shape
    panel = diag_inverses.shape[1]
    own_x, own_y = residual.shape
    chunks = columns // CHUNK
    devices = R * C
    any_spec = pl.BlockSpec(memory_space=pl.ANY)
    vmem = pl.BlockSpec(memory_space=pltpu.VMEM)
    dma = pltpu.SemaphoreType.DMA
    ready = columns
    held_shape = (2, C, low_factor.shape[1], panel)
    partial, upper_in, smoothed_in, coarse_in = pl.pallas_call(
        functools.partial(kernel, R, C),
        out_shape=(
            jax.ShapeDtypeStruct((rows, ready), BF16),
            jax.ShapeDtypeStruct((2, panel, columns), BF16),
            jax.ShapeDtypeStruct((own_x, own_y), F32),
            jax.ShapeDtypeStruct((1, COARSE_DEV), F32),
        ),
        in_specs=[any_spec] * 12,
        out_specs=[any_spec] * 4,
        scratch_shapes=[
            pltpu.VMEM((2, panel, panel), BF16),
            pltpu.VMEM((panel, panel), BF16),
            pltpu.VMEM(pivots.shape, jnp.int32),
            pltpu.VMEM((own_x, own_y), F32),
            pltpu.VMEM((own_x, own_y), F32),
            pltpu.VMEM((own_x, own_y), F32),
            pltpu.VMEM(basis_cells.shape[1:], jnp.int32),
            pltpu.VMEM(basis_cells.shape[1:], F32),
            pltpu.VMEM(basis_cells.shape[1:], jnp.int32),
            pltpu.VMEM((own_x, own_y), F32),
            pltpu.VMEM((1, COARSE_DEV), F32),
            pltpu.VMEM((chunks, 2, panel, CHUNK), BF16),
            pltpu.VMEM(held_shape, BF16),
            pltpu.VMEM((rows, ready), BF16),
            pltpu.VMEM((2, panel, columns), BF16),
            pltpu.VMEM((2, panel, panel), BF16),
            pltpu.VMEM((own_x + 32, own_y + 256), F32),
            pltpu.VMEM((own_x + 32, own_y + 256), F32),
            pltpu.VMEM((own_x + 32, own_y + 256), F32),
            pltpu.VMEM((2, 2, 8, own_y), F32),
            pltpu.VMEM((2, 2, 8, own_y), F32),
            pltpu.VMEM((4, own_x + 16, 128), F32),
            pltpu.VMEM((3 * own_x, own_y), BF16),
            pltpu.VMEM((C, R, 1, 128), F32),
            pltpu.VMEM((C, R, 1, 128), F32),
            pltpu.VMEM((devices, 1, 128), F32),
            dma((2, R - 1, chunks)),
            dma((2, R - 1, chunks)),
            dma((2, C)),
            dma((2, C)),
            dma((2,)),
            dma((2,)),
            dma((2,)),
            dma((2,)),
            dma((C,)),
            dma((C,)),
            dma((R,)),
            dma((R,)),
            dma((3,)),
            dma((chunks,)),
            dma((chunks,)),
            dma((chunks,)),
            dma((9,)),
            dma((2,)),
        ],
        compiler_params=pltpu.CompilerParams(
            collective_id=0, has_side_effects=True, vmem_limit_bytes=56 * 1024 * 1024
        ),
        cost_estimate=pl.CostEstimate(
            flops=2 * rows * columns * 2 * panel, bytes_accessed=4 * rows * columns,
            transcendentals=0,
        ),
    )(
        trailing, low_factor, panel_tops, diag_inverses, link_rows, pivots, residual, diagonal,
        coupling, basis_cells[0], basis_weights[0], coarse_slots[0],
    )
    updated, upper_rows, smoothed, coarse = pl.pallas_call(
        finish,
        out_shape=(
            jax.ShapeDtypeStruct((rows, columns), BF16),
            jax.ShapeDtypeStruct((2, panel, columns), BF16),
            jax.ShapeDtypeStruct((own_x, own_y), F32),
            jax.ShapeDtypeStruct((COARSE_DEV,), F32),
        ),
        in_specs=[any_spec] * 3 + [vmem],
        out_specs=[any_spec] * 3 + [vmem],
        scratch_shapes=[
            pltpu.VMEM((rows, ready), BF16),
            pltpu.VMEM((2, panel, columns), BF16),
            pltpu.VMEM((own_x, own_y), F32),
            dma((PARTS + 3,)),
            dma((PARTS + 3,)),
        ],
        compiler_params=pltpu.CompilerParams(vmem_limit_bytes=56 * 1024 * 1024),
    )(partial, upper_in, smoothed_in, coarse_in)
    return updated, upper_rows, smoothed, coarse


def solution(mesh):
    return jax.shard_map(
        functools.partial(shards, mesh.shape["row"], mesh.shape["col"]),
        mesh=mesh,
        in_specs=(
            P("row", "col"),
            P(None, ("row", "col"), None),
            P(None, "row", "col"),
            P(),
            P(),
            P(),
            P("row", "col"),
            P("row", "col"),
            P("row", "col"),
            P(("row", "col"), None, None),
            P(("row", "col"), None, None),
            P(("row", "col"), None, None),
        ),
        out_specs=(P("row", "col"), P(None, None, "col"), P("row", "col"), P(("row", "col"))),
        check_vma=False,
    )
```
